32 devices in a mesh: ex: 2 (over core), slab: 16 (over z, y, x).
Axes of the slice: x: 2, y: 2, z: 4, core: 2. Of those that a mesh axis runs over, the one named last changes fastest.
Arguments:
- volume: bfloat16 [2, 16, 128, 32, 128], P('ex', None, 'slab'), may hold values from -6 to 6
- cotangent: bfloat16 [2, 16, 128, 32, 128], P('ex', None, 'slab')
- gate_mask: int32 [2, 2, 128, 32, 128], P('ex', None, 'slab'), may hold values 0 or 1
- loss_scale: float32 [2], P('ex'), may hold values from 0.05 to 5
- canary: int32 [2], P('ex'), may hold values from 0 to 15
- kernels: bfloat16 [2, 32, 432], replicated, may hold values from -0.3125 to 0.3125
Outputs:
- input_grad: float32 [2, 16, 128, 32, 128], P('ex', None, 'slab')
- kernel_grad: float32 [2, 32, 432], replicated
The draws below stay inside these ranges and needn't reach their ends.
All inputs are finite; a program needn't handle non-finite values. No bound on the sum of `gate_mask` on one device may be relied on, other than what follows from the above.
Results may differ from the reference program's by a relative error of at most 0.0037.
Values may be sent and summed in bfloat16 or wider, within the bound.
No kernel may reach another device: no remote copies, remote signals or barrier semaphores. Data moves between devices by JAX's collectives and lax.ppermute only.
A program may use at most 192 MiB of HBM per device.

```python
import math
import jax
import jax.numpy as jnp
from jax import lax

C = 16
DEPTH = 128
H = 32
W = 128
EX = 2


def draw_cotangent(key, part):
    key_base = jax.random.fold_in(key, 11)
    key_chan = jax.random.fold_in(key, 12)
    base = jax.random.normal(key_base, (EX, C, DEPTH, H, W), jnp.float32)
    base = jnp.clip(base, -4.0, 4.0)
    chan_scale = jnp.exp(jax.random.uniform(key_chan, (EX, C, 1, 1, 1), jnp.float32, jnp.log(0.5), jnp.log(5.0)))
    return (base * chan_scale * 0.3).astype(jnp.bfloat16)


def place_ends(result, rng, smallest, top_value):
    longest = result.shape.index(max(result.shape))
    spots = []
    for shift in (0, 1):
        where = [jax.random.randint(jax.random.fold_in(rng, axis), (), 0, length) for axis, length in enumerate(result.shape)]
        where[longest] = (where[longest] + shift) % result.shape[longest]
        spots.append(tuple(where))
    return result.at[spots[0]].set(smallest).at[spots[1]].set(top_value)


def block_levels(rng, extent, split, low, largest):
    loudness, own = 1.0, jax.random.fold_in(rng, 6)
    for dim, parts in split:
        steps = jnp.exp(jax.random.uniform(jax.random.fold_in(own, dim), (parts,), jnp.float32, low / len(split), largest / len(split)))
        loudness = loudness * jnp.repeat(steps, extent[dim] // parts).reshape([-1 if axis == dim else 1 for axis in range(len(extent))])
    return loudness


def normal_values(own_key, dims, spread, reach, shards=(), kind=jnp.bfloat16):
    values = jax.random.normal(own_key, dims, jnp.float32) * spread
    if len(shards) > 0:
        values = block_levels(own_key, dims, shards, -0.22, 0.18) * values
    return jnp.clip(values, min=-reach, max=reach).astype(kind)


def setup_inputs(seed: int = 0) -> dict:
    seeds = jax.random.split(jax.random.key(seed), 7)
    volume = normal_values(seeds[0], (EX, C, DEPTH, H, W), 1.0, 6.0, ((0, 2), (2, 16)))
    cotangent = draw_cotangent(jax.random.fold_in(seeds[6], 71), 0)
    gate_mask = place_ends((jax.random.randint(seeds[2], (EX, 2, DEPTH, H, W), 0, 4) < 3).astype(jnp.int32), jax.random.fold_in(seeds[2], 1), 0, 1)
    loss_scale = jnp.clip(jnp.exp(math.log(5.0) - 4.6051702 * jax.random.uniform(seeds[3], (EX,), jnp.float32) ** block_levels(seeds[3], (EX,), ((0, 2),), -0.2, 0.2)), 0.05, 5.0)
    canary = jax.random.randint(seeds[4], (EX,), 0, C).astype(jnp.int32)
    kernels = normal_values(seeds[5], (2, 2 * C, 27 * C), (27 * C) ** -0.5, 0.3125)
    return dict(volume=volume, cotangent=cotangent, gate_mask=gate_mask, loss_scale=loss_scale, canary=canary, kernels=kernels)


def columns(field):
    zs, hs, ws = (field.shape[1], field.shape[2], field.shape[3])
    padded = jnp.pad(field, ((0, 0), (1, 1), (1, 1), (1, 1)))
    taps = []
    for dz in range(3):
        for dh in range(3):
            for dw in range(3):
                taps.append(padded[:, dz:dz + zs, dh:dh + hs, dw:dw + ws])
    stacked = jnp.stack(taps, axis=0)
    return stacked.reshape((27 * field.shape[0], zs, hs, ws))

def back_columns(field):
    zs, hs, ws = (field.shape[1], field.shape[2], field.shape[3])
    padded = jnp.pad(field, ((0, 0), (1, 1), (1, 1), (1, 1)))
    taps = []
    for dz in range(3):
        for dh in range(3):
            for dw in range(3):
                taps.append(padded[:, 2 - dz:2 - dz + zs, 2 - dh:2 - dh + hs, 2 - dw:2 - dw + ws])
    return jnp.stack(taps, axis=0)

def forward_conv(kernel, field):
    return jnp.einsum('ok,kzhw->ozhw', kernel.astype(jnp.float32), columns(field).astype(jnp.float32))

def transposed_conv(kernel, grads):
    shaped = kernel.astype(jnp.float32).reshape((2 * C, 27, C))
    return jnp.einsum('otc,tozhw->czhw', shaped, back_columns(grads).astype(jnp.float32))

def kernel_product(grads, field):
    return jnp.einsum('ozhw,kzhw->ok', grads.astype(jnp.float32), columns(field).astype(jnp.float32))

def one_example(volume, cotangent, gate_mask, loss_scale, canary, kernels):
    mask_one = gate_mask[0].astype(jnp.float32)
    mask_two = gate_mask[1].astype(jnp.float32)
    pre_one = forward_conv(kernels[0], volume)
    value_one = pre_one[:C]
    sig_one = jax.nn.sigmoid(pre_one[C:])
    hidden = (volume.astype(jnp.float32) + value_one * sig_one * mask_one).astype(jnp.bfloat16)
    pre_two = forward_conv(kernels[1], hidden)
    value_two = pre_two[:C]
    sig_two = jax.nn.sigmoid(pre_two[C:])
    weights = 1.0 + 2.0 * (jnp.arange(C, dtype=jnp.int32) == canary).astype(jnp.float32)
    grad_out = cotangent.astype(jnp.float32) * loss_scale * weights[:, None, None, None]
    delta_two = jnp.concatenate([grad_out * sig_two * mask_two, grad_out * value_two * sig_two * (1.0 - sig_two) * mask_two], axis=0).astype(jnp.bfloat16)
    grad_two = kernel_product(delta_two, hidden)
    grad_hidden = grad_out + transposed_conv(kernels[1], delta_two)
    delta_one = jnp.concatenate([grad_hidden * sig_one * mask_one, grad_hidden * value_one * sig_one * (1.0 - sig_one) * mask_one], axis=0).astype(jnp.bfloat16)
    grad_one = kernel_product(delta_one, volume)
    input_grad = grad_hidden + transposed_conv(kernels[0], delta_one)
    stacked = jnp.stack([grad_one, grad_two], axis=0)
    norm = jnp.sqrt(jnp.sum(stacked * stacked) + 1e-06)
    bound = 20.0 * jnp.sqrt(jnp.float32(DEPTH * H * W))
    factor = jnp.minimum(1.0, bound / norm)
    return (input_grad, stacked * factor)

def reference(volume, cotangent, gate_mask, loss_scale, canary, kernels):

    def single(items):
        return one_example(items[0], items[1], items[2], items[3], items[4], kernels)
    input_grad, clipped = lax.map(single, (volume, cotangent, gate_mask, loss_scale, canary))
    bound = 20.0 * jnp.sqrt(jnp.float32(DEPTH * H * W))
    scaling = jnp.sqrt(jnp.float32(108 * C * C)) / (bound * jnp.sqrt(jnp.float32(EX)))
    kernel_grad = lax.optimization_barrier(jnp.sum(clipped, axis=0)) * scaling
    return (input_grad, kernel_grad)
```

```python
import functools
import jax
import jax.numpy as jnp
from jax import lax
from jax.experimental import pallas as pl
from jax.experimental.pallas import tpu as pltpu
from jax.sharding import PartitionSpec as P

F32, BF16 = jnp.float32, jnp.bfloat16
PZ, PH = 2, 4
WZ, WH = PZ + 2, PH + 2
VMEM = pltpu.VMEM


def with_halo(array, sides, width):
    for axis, dim in sides:
        peers, length = (lax.axis_size(axis), array.shape[dim])
        up = [(i, (i + 1) % peers) for i in range(peers - 1)]
        down = [(j, i) for i, j in up]
        last = lax.slice_in_dim(array, length - width, length, axis=dim)
        leading = lax.slice_in_dim(array, 0, width, axis=dim)
        before = lax.ppermute(last, axis, up)
        after = lax.ppermute(leading, axis, down)
        array = jnp.concatenate([before, array, after], axis=dim)
    return array


def shifted_stack(extended, flip):
    zs = extended.shape[2] - 2
    hs, ws = (extended.shape[3], extended.shape[4])
    padded = jnp.pad(extended, ((0, 0), (0, 0), (0, 0), (1, 1), (1, 1)))
    taps = []
    for tap in range(27):
        dz, dh, dw = tap // 9, tap // 3 % 3, tap % 3
        if flip:
            dz, dh, dw = 2 - dz, 2 - dh, 2 - dw
        taps.append(padded[:, :, dz : dz + zs, dh : dh + hs, dw : dw + ws])
    return jnp.stack(taps, axis=1)


def layer_forward(field, kernel):
    patches = shifted_stack(with_halo(field, (("slab", 2),), 1), False)
    ex, taps, chans, zs, hs, ws = patches.shape
    patches = patches.reshape((ex, taps * chans, zs, hs, ws))
    pre = jnp.einsum("ok,ekzhw->eozhw", kernel, patches, preferred_element_type=F32)
    return (pre, patches)


def layer_backward(delta, kernel, patches):
    grads = jnp.einsum("eozhw,ekzhw->eok", delta, patches, preferred_element_type=F32)
    extended = with_halo(delta, (("slab", 2),), 1)
    shaped = kernel.reshape((kernel.shape[0], 27, kernel.shape[1] // 27))
    spread = jnp.einsum(
        "otc,etozhw->eczhw", shaped, shifted_stack(extended, True), preferred_element_type=F32
    )
    return (grads, spread)


def plain_device(volume, cotangent, gate_mask, loss_scale, canary, kernels):
    chans = volume.shape[1]
    local_ex = volume.shape[0]
    mask_one = gate_mask[:, 0][:, None].astype(F32)
    mask_two = gate_mask[:, 1][:, None].astype(F32)
    pre_one, patches_one = layer_forward(volume, kernels[0])
    value_one = pre_one[:, :chans]
    sig_one = jax.nn.sigmoid(pre_one[:, chans:])
    hidden = (volume.astype(F32) + value_one * sig_one * mask_one).astype(BF16)
    pre_two, patches_two = layer_forward(hidden, kernels[1])
    value_two = pre_two[:, :chans]
    sig_two = jax.nn.sigmoid(pre_two[:, chans:])
    weights = channel_weights(chans, loss_scale, canary)
    grad_out = cotangent.astype(F32) * weights[:, :, None, None, None]
    delta_two = jnp.concatenate(
        [
            grad_out * sig_two * mask_two,
            grad_out * value_two * sig_two * (1.0 - sig_two) * mask_two,
        ],
        axis=1,
    ).astype(BF16)
    grad_two, spread_two = layer_backward(delta_two, kernels[1], patches_two)
    grad_hidden = grad_out + spread_two
    delta_one = jnp.concatenate(
        [
            grad_hidden * sig_one * mask_one,
            grad_hidden * value_one * sig_one * (1.0 - sig_one) * mask_one,
        ],
        axis=1,
    ).astype(BF16)
    grad_one, spread_one = layer_backward(delta_one, kernels[0], patches_one)
    input_grad = grad_hidden + spread_one
    flat = jnp.stack([grad_one, grad_two], axis=1).reshape((local_ex, -1))
    bound, scaling = clip_numbers(volume, kernels)
    summed = lax.psum(flat, "slab")
    norm = jnp.sqrt(jnp.sum(summed * summed, axis=1) + 1e-06)
    factor = jnp.minimum(1.0, bound / norm)
    total = lax.psum(jnp.sum(summed * factor[:, None], axis=0), "ex")
    return (input_grad, (total * scaling).reshape(kernels.shape))


def channel_weights(chans, loss_scale, canary):
    ids = jnp.arange(chans, dtype=jnp.int32)
    return (1.0 + 2.0 * (ids[None, :] == canary[:, None]).astype(F32)) * loss_scale[:, None]


def clip_numbers(volume, kernels):
    chans = volume.shape[1]
    depth = volume.shape[2] * lax.axis_size("slab")
    bound = 20.0 * jnp.sqrt(F32(depth * volume.shape[3] * volume.shape[4]))
    examples = volume.shape[0] * lax.axis_size("ex")
    scaling = jnp.sqrt(F32(108 * chans * chans)) / (bound * jnp.sqrt(F32(examples)))
    return bound, scaling


def side_shifts(tile):
    lane = lax.broadcasted_iota(jnp.int32, tile.shape, tile.ndim - 1)
    last = tile.shape[-1] - 1
    before = jnp.where(lane == 0, 0.0, pltpu.roll(tile, 1, tile.ndim - 1))
    after = jnp.where(lane == last, 0.0, pltpu.roll(tile, last, tile.ndim - 1))
    return before, after


def put_rows(ref, plane, h, tile):
    rows, chans = tile.shape[:2]
    before, after = side_shifts(tile)
    for s, part in enumerate((before, tile, after)):
        ref[plane, pl.ds(h + 1, rows), s * chans : (s + 1) * chans, :] = part.astype(BF16)


def put_pair_rows(ref, plane, h, top, low):
    rows, chans = top.shape[:2]
    for first, tile in ((0, top), (chans, low)):
        before, after = side_shifts(tile)
        for s, part in enumerate((before, tile, after)):
            at = s * 2 * chans + first
            ref[plane, pl.ds(h + 1, rows), at : at + chans, :] = part.astype(BF16)


def clear_edges(ref):
    for plane in range(ref.shape[0]):
        zero = jnp.zeros(ref.shape[2:], BF16)
        ref[plane, 0] = zero
        ref[plane, ref.shape[1] - 1] = zero


def windows(planes, blocks):
    cols = []
    for h in blocks:
        parts = []
        for ref, at in planes:
            part = ref[at, pl.ds(h, WH)]
            parts.append(part.reshape((-1, part.shape[-1])))
        cols.append(jnp.concatenate(parts, axis=0))
    return jnp.concatenate(cols, axis=1)


def conv_blocks(mat, planes, h):
    out = jnp.dot(mat, windows(planes, (h, h + PH)), preferred_element_type=F32)
    return out.reshape((PZ * PH, -1, out.shape[-1]))


def split_blocks(tile, fn):
    half = tile.shape[-1] // 2
    for pz in range(PZ):
        for b in range(2):
            fn(pz, b, tile[pz * PH : (pz + 1) * PH, :, b * half : (b + 1) * half])


def join_blocks(fn):
    return jnp.concatenate(
        [jnp.concatenate([fn(pz, 0), fn(pz, 1)], axis=2) for pz in range(PZ)], axis=0
    )


def mask_blocks(mask_planes, h, chans):
    parts = []
    for pz in range(PZ):
        ref, at = mask_planes[pz]
        rows = ref[at + (pl.ds(h, 2 * PH),)].astype(F32)
        both = jnp.concatenate([rows[:PH], rows[PH:]], axis=1)
        parts.append(jnp.broadcast_to(both[:, None, :], (PH, chans, both.shape[1])))
    return jnp.concatenate(parts, axis=0)


def row_loop(hs, body):
    def step(i, carry):
        body(pl.multiple_of(i * (2 * PH), 2 * PH))
        return carry

    lax.fori_loop(0, hs // (2 * PH), step, 0)


def forward_one(mat_ref, v_planes, v_centre, mask_planes, x1, x1_at, gates, gates_at, hs, chans):
    def body(h):
        pre = conv_blocks(mat_ref[...], v_planes, h)
        val, sig = pre[:, :chans], jax.nn.sigmoid(pre[:, chans:])
        mask = mask_blocks(mask_planes, h, chans)

        def centre(pz, b):
            ref, at = v_centre[pz]
            return ref[at, pl.ds(h + b * PH + 1, PH), chans : 2 * chans, :].astype(F32)

        open_ = sig * mask
        hid = join_blocks(centre) + val * open_
        slope = val * open_ * (1.0 - sig)
        split_blocks(hid, lambda pz, b, t: put_rows(x1, x1_at + pz, h + b * PH, t))

        def keep(which):
            def put(pz, b, t):
                gates[which, gates_at + pz, pl.ds(h + b * PH, PH)] = t

            return put

        split_blocks(open_, keep(0))
        split_blocks(slope, keep(1))

    row_loop(hs, body)


def forward_two(mat_ref, x1_planes, mask_planes, dy_fn, d2, d2_at, hs, chans):
    def body(h):
        pre = conv_blocks(mat_ref[...], x1_planes, h)
        val, sig = pre[:, :chans], jax.nn.sigmoid(pre[:, chans:])
        dy = join_blocks(lambda pz, b: dy_fn(pz, h + b * PH))
        top = dy * sig * mask_blocks(mask_planes, h, chans)
        low = top * val * (1.0 - sig)
        half = top.shape[-1] // 2
        for pz in range(PZ):
            for b in range(2):
                at = (slice(pz * PH, (pz + 1) * PH), slice(None), slice(b * half, (b + 1) * half))
                put_pair_rows(d2, d2_at + pz, h + b * PH, top[at], low[at])

    row_loop(hs, body)


def backward_two(mat, d2_planes, dy_fn, gates, gates_at, dx, dx_at, d1, d1_at, hs):
    def body(h):
        spread = conv_blocks(mat(), d2_planes, h)
        half = spread.shape[-1] // 2
        for pz in range(PZ):
            for b in range(2):
                row = h + b * PH
                part = spread[pz * PH : (pz + 1) * PH, :, b * half : (b + 1) * half]
                if dy_fn[pz] is not None:
                    part = part + dy_fn[pz](row)
                dx[dx_at + pz, pl.ds(row, PH)] = part
                put_pair_rows(
                    d1,
                    d1_at + pz,
                    row,
                    part * gates[0, gates_at + pz, pl.ds(row, PH)],
                    part * gates[1, gates_at + pz, pl.ds(row, PH)],
                )

    row_loop(hs, body)


def weight_blocks(x_planes, d_planes, acc, hs):
    blocks = tuple(range(0, hs, PH))
    lhs = windows(x_planes, blocks)
    cols = []
    for h in blocks:
        parts = []
        for ref, at in d_planes:
            outs = ref.shape[2] // 3
            parts.append(ref[at, h + 1 : h + 1 + PH, outs : 2 * outs, :].reshape((PH * outs, -1)))
        cols.append(jnp.concatenate(parts, axis=0))
    rhs = jnp.concatenate(cols, axis=1)
    acc[...] += lax.dot_general(lhs, rhs, (((1,), (1,)), ((), ())), preferred_element_type=F32)


def fold_blocks(acc, outs, chans):
    taps = 9 * chans
    width = PH * outs
    rows = WH * 3 * chans
    total = None
    for ph in range(PH):
        part = None
        for pz in range(PZ):
            pieces = []
            for dz in range(3):
                at = (pz + dz) * rows + ph * 3 * chans
                pieces.append(acc[at : at + taps, pz * width : (pz + 1) * width])
            piece = jnp.concatenate(pieces, axis=0)
            part = piece if part is None else part + piece
        if ph:
            part = pltpu.roll(part, width - ph * outs, 1)
        total = part if total is None else total + part
    return total


def place_matrix(cols, stride, total, piece):
    k = lax.broadcasted_iota(jnp.int32, (cols, total), 0)
    j = lax.broadcasted_iota(jnp.int32, (cols, total), 1)
    group = (k >= piece).astype(jnp.int32) + (k >= 2 * piece).astype(jnp.int32)
    return (j == k + group * (stride - piece)).astype(F32).astype(BF16)


def spread_kernel(rows, out_ref, layer, width):
    outs, cols = rows.shape
    stride = WH * width
    place = place_matrix(cols, stride, WZ * stride, 3 * width)
    base = jnp.dot(rows, place, preferred_element_type=F32)
    for pz in range(PZ):
        for ph in range(PH):
            at = (pz * PH + ph) * outs
            shift = pz * stride + ph * width
            tile = pltpu.roll(base, shift, 1) if shift else base
            out_ref[layer, at : at + outs, :] = tile.astype(BF16)


def to_rows(source, scratch, put):
    chans, hs, ws = source.shape
    scratch[...] = source.astype(F32).reshape((chans * hs, ws))
    for h in range(hs):
        put(h, scratch[pl.ds(h, chans, stride=hs), :])


def inner_kernel(zs, vol, cot, mask, wts, ker, kft, mf, mb, xv, ct, x1, g1, d2, dx, d1, t1, t2, rows):
    chans, hs = vol.shape[0], vol.shape[2]
    for layer in range(2):
        spread_kernel(ker[layer], mf, layer, 3 * chans)
        spread_kernel(kft[layer], mb, layer, 6 * chans)
    for ref in (xv, x1, d2, d1):
        clear_edges(ref)

    def arrange(z, carry):
        to_rows(vol[:, z], rows, lambda h, t: put_rows(xv, z, h, t[None]))

        def put(h, t):
            ct[z, h] = (t * wts[...]).astype(F32)

        to_rows(cot[:, z], rows, put)
        return carry

    lax.fori_loop(0, zs, arrange, 0)

    def layer_one(k, carry):
        z = 2 * k + 1
        forward_one(
            mf.at[0],
            [(xv, z - 1 + i) for i in range(WZ)],
            [(xv, z + i) for i in range(PZ)],
            [(mask, (0, z + i)) for i in range(PZ)],
            x1, 2 * k, g1, 2 * k, hs, chans,
        )
        return carry

    lax.fori_loop(0, (zs - 2) // 2, layer_one, 0)
    t1[...] = jnp.zeros_like(t1)
    t2[...] = jnp.zeros_like(t2)

    def layer_two(k, carry):
        z = 2 * k + 2
        x_planes = [(x1, z - 2 + i) for i in range(WZ)]
        forward_two(
            mf.at[1], x_planes, [(mask, (1, z + i)) for i in range(PZ)],
            lambda pz, h: ct[z + pz, pl.ds(h, PH)], d2, 2 * k, hs, chans,
        )
        weight_blocks(x_planes, [(d2, 2 * k + i) for i in range(PZ)], t2, hs)
        return carry

    lax.fori_loop(0, (zs - 4) // 2, layer_two, 0)

    def layer_back(k, carry):
        z = 2 * k + 3
        dys = [lambda h, i=i: ct[z + i, pl.ds(h, PH)] for i in range(PZ)]
        backward_two(
            lambda: mb[1], [(d2, z - 3 + i) for i in range(WZ)], dys, g1, z - 1, dx, 2 * k, d1, 2 * k, hs
        )
        weight_blocks(
            [(xv, z - 1 + i) for i in range(WZ)], [(d1, 2 * k + i) for i in range(PZ)], t1, hs
        )
        return carry

    lax.fori_loop(0, (zs - 6) // 2, layer_back, 0)


def edge_kernel(low, halo, xv, x1, d2, gates, mask, ct, mf, mb,
                send, dx, d1, t1, t2, xh, x1h, d2h, gh, rows):
    chans, hs = xv.shape[2] // 3, xv.shape[1] - 2
    for ref in (xh, x1h, d2h, d1):
        clear_edges(ref)
    for i in range(2):
        to_rows(halo[i * chans : (i + 1) * chans], rows, lambda h, t: put_rows(xh, i, h, t[None]))
    outer = (halo, (2 * chans,))
    if low:
        v_planes = [(xh, 0), (xh, 1), (xv, 0), (xv, 1)]
        v_centre = [(xh, 1), (xv, 0)]
        masks1 = [outer, (mask, (0, 0))]
        masks2 = [(mask, (1, 0)), (mask, (1, 1))]
        x_planes = [(x1h, 0), (x1h, 1), (x1, 0), (x1, 1)]
        d_edge = [(d2h, 0), (d2h, 1)]
        half = slice(mb.shape[2] // 2, mb.shape[2])
        dy_edge = [None, lambda h: ct[0, pl.ds(h, PH)]]
        d_next = [(d2h, 0), (d2h, 1), (d2, 0), (d2, 1)]
        dy_next = [lambda h, i=i: ct[1 + i, pl.ds(h, PH)] for i in range(2)]
        at_edge, at_next, base = 0, 2, 0
        dy_two = lambda pz, h: ct[pz, pl.ds(h, PH)]
        v_next = [(xv, i) for i in range(4)]
    else:
        v_planes = [(xv, 2), (xv, 3), (xh, 0), (xh, 1)]
        v_centre = [(xv, 3), (xh, 0)]
        masks1 = [(mask, (0, 3)), outer]
        masks2 = [(mask, (1, 2)), (mask, (1, 3))]
        x_planes = [(x1, 0), (x1, 1), (x1h, 0), (x1h, 1)]
        d_edge = [(d2h, 0), (d2h, 1)]
        half = slice(0, mb.shape[2] // 2)
        dy_edge = [lambda h: ct[3, pl.ds(h, PH)], None]
        d_next = [(d2, 0), (d2, 1), (d2h, 0), (d2h, 1)]
        dy_next = [lambda h, i=i: ct[1 + i, pl.ds(h, PH)] for i in range(2)]
        at_edge, at_next, base = 2, 0, 0
        dy_two = lambda pz, h: ct[2 + pz, pl.ds(h, PH)]
        v_next = [(xv, i) for i in range(4)]
    forward_one(mf.at[0], v_planes, v_centre, masks1, x1h, 0, gh, 0, hs, chans)
    forward_two(mf.at[1], x_planes, masks2, dy_two, d2h, 0, hs, chans)
    backward_two(lambda: mb[1, :, half], d_edge, dy_edge, gh, 0, dx, at_edge, d1, at_edge, hs)

    outside = 0 if low else 1

    def spread(h):
        out = conv_blocks(mb[0, :, half], [(d1, at_edge), (d1, at_edge + 1)], h)
        width = out.shape[-1] // 2
        for pz in range(PZ):
            for b in range(2):
                row = h + b * PH
                part = out[pz * PH : (pz + 1) * PH, :, b * width : (b + 1) * width]
                if pz == 1 - outside:
                    part = part + dx[at_edge + outside, pl.ds(row, PH)]
                send[pz, pl.ds(row, PH)] = part.astype(BF16)

    row_loop(hs, spread)
    t1[...] = jnp.zeros_like(t1)
    t2[...] = jnp.zeros_like(t2)
    weight_blocks(x_planes, [(d2h, 0), (d2h, 1)], t2, hs)
    weight_blocks(v_planes, [(d1, at_edge + i) for i in range(2)], t1, hs)
    backward_two(lambda: mb[1], d_next, dy_next, gates, 0, dx, at_next, d1, at_next, hs)
    weight_blocks(v_next, [(d1, at_next + i) for i in range(2)], t1, hs)


def fold_kernel(a1, a2, b1, b2, c1, c2, out, acc):
    chans = a1.shape[0] // (WZ * WH * 3)
    outs = 2 * chans
    acc[...] = a1[...] + b1[...] + c1[...]
    one = fold_blocks(acc, outs, chans)
    acc[...] = a2[...] + b2[...] + c2[...]
    two = fold_blocks(acc, outs, chans)
    lane = lax.broadcasted_iota(jnp.int32, one.shape, 1)
    both = jnp.where(lane < outs, one, pltpu.roll(two, outs, 1))
    half = both.shape[0] // 2
    lane = lax.broadcasted_iota(jnp.int32, (half, both.shape[1]), 1)
    out[...] = jnp.where(lane < 2 * outs, both[:half], pltpu.roll(both[half:], 2 * outs, 1))


def output_kernel(zs, mb, d1a, d1b, d1c, dxa, dxb, dxc, lo, hi, out, rows):
    chans, hs, ws = out.shape[0], out.shape[2], out.shape[3]

    def plane_of(refs, z):
        if z <= 2:
            return (refs[0], z + 1)
        if z <= zs - 4:
            return (refs[1], z - 3)
        return (refs[2], z - (zs - 3))

    for z in range(0, zs, 2):
        planes = [plane_of((d1a, d1b, d1c), z - 1 + i) for i in range(WZ)]
        dxs = [plane_of((dxa, dxb, dxc), z + i) for i in range(PZ)]
        extra = lo if z == 0 else hi if z == zs - 2 else None

        def body(h):
            res = conv_blocks(mb[0], planes, h)
            width = res.shape[-1] // 2
            for pz in range(PZ):
                for b in range(2):
                    row = h + b * PH
                    part = res[pz * PH : (pz + 1) * PH, :, b * width : (b + 1) * width]
                    ref, at = dxs[pz]
                    part = part + ref[at, pl.ds(row, PH)]
                    if extra is not None:
                        part = part + extra[pz, pl.ds(row, PH)].astype(F32)
                    at = pl.multiple_of(row * chans, chans)
                    rows[pz, pl.ds(at, PH * chans), :] = part.reshape((PH * chans, ws))

        row_loop(hs, body)
        for pz in range(PZ):
            for c in range(chans):
                out[c, z + pz] = rows[pz, pl.ds(c, hs, stride=chans), :]


def clip_kernel(mine, other, bound, scaling, out):
    total = None
    for ref in (mine, other):
        value = ref[...]
        norm = jnp.sqrt(jnp.sum(value * value, keepdims=True) + 1e-06)
        part = value * jnp.minimum(1.0, bound[...] / norm)
        total = part if total is None else total + part
    total = total * scaling[...]
    outs = out.shape[1]
    half = total.shape[0]
    flat = total.T
    for layer in range(2):
        for part in range(2):
            at = (part * 2 + layer) * outs
            out[layer, :, part * half : (part + 1) * half] = flat[at : at + outs]


def call(body, outs, scratch=(), flops=0, vmem=56 << 20):
    def run(*args):
        size = sum(a.size * a.dtype.itemsize for a in args) + sum(o.size * o.dtype.itemsize for o in outs)
        return pl.pallas_call(
            body,
            out_shape=outs,
            scratch_shapes=list(scratch),
            compiler_params=pltpu.CompilerParams(vmem_limit_bytes=vmem),
            cost_estimate=pl.CostEstimate(flops=flops, bytes_accessed=size, transcendentals=0),
        )(*args)

    return run


def shape(*dims, dtype=F32):
    return jax.ShapeDtypeStruct(dims, dtype)


def sum_over_slab(value):
    peers = lax.axis_size("slab")
    step = 1
    order = []
    while step < peers:
        order.append(step)
        step *= 2
    for step in order[1:] + order[:1]:
        value = value + lax.ppermute(value, "slab", [(i, i ^ step) for i in range(peers)])
    return value


def block_device(volume, cotangent, gate_mask, loss_scale, canary, kernels):
    chans, zs, hs, ws = volume.shape[1:]
    outs = 2 * chans
    vol, cot, mask = volume[0], cotangent[0], gate_mask[0]
    peers = lax.axis_size("slab")
    up = [(i, i + 1) for i in range(peers - 1)]
    down = [(i + 1, i) for i in range(peers - 1)]

    def packed(first, edge):
        planes = [vol[:, first], vol[:, first + 1], mask[0, edge][None].astype(BF16)]
        return jnp.concatenate(planes, axis=0)

    below = lax.ppermute(packed(zs - 2, zs - 1), "slab", up)
    above = lax.ppermute(packed(0, 0), "slab", down)

    wts = jnp.broadcast_to(channel_weights(chans, loss_scale, canary)[0][:, None], (chans, ws))
    kft = kernels.reshape((2, outs, 27, chans))[:, :, ::-1].transpose((0, 3, 2, 1))
    kft = kft.reshape((2, chans, 27 * outs))

    k_fwd, k_bwd = WZ * WH * 3 * chans, WZ * WH * 3 * outs
    m_fwd, m_bwd = PZ * PH * outs, PZ * PH * chans
    x_plane, d_plane, c_plane = (hs + 2, 3 * chans, ws), (hs + 2, 3 * outs, ws), (hs, chans, ws)
    acc = shape(k_fwd, m_fwd)
    rows = VMEM((chans * hs, ws), F32)
    pair = 2 * k_fwd * m_fwd * hs // PH * ws

    mf, mb, xv, ct, x1, g1, d2, dx_in, d1_in, t1_in, t2_in = call(
        functools.partial(inner_kernel, zs),
        [
            shape(2, m_fwd, k_fwd, dtype=BF16),
            shape(2, m_bwd, k_bwd, dtype=BF16),
            shape(zs, *x_plane, dtype=BF16),
            shape(zs, *c_plane),
            shape(zs - 2, *x_plane, dtype=BF16),
            shape(2, zs - 2, *c_plane),
            shape(zs - 4, *d_plane, dtype=BF16),
            shape(zs - 6, *c_plane),
            shape(zs - 6, *d_plane, dtype=BF16),
            acc,
            acc,
        ],
        [rows],
        flops=pair * 10,
    )(vol, cot, mask, wts, kernels, kft)

    def edge(low, halo):
        four = slice(0, 4) if low else slice(zs - 4, zs)
        two = slice(0, 2) if low else slice(zs - 4, zs - 2)
        two_d = slice(0, 2) if low else slice(zs - 6, zs - 4)
        return call(
            functools.partial(edge_kernel, low),
            [
                shape(2, *c_plane, dtype=BF16),
                shape(4, *c_plane),
                shape(4, *d_plane, dtype=BF16),
                acc,
                acc,
            ],
            [
                VMEM((2,) + x_plane, BF16),
                VMEM((2,) + x_plane, BF16),
                VMEM((2,) + d_plane, BF16),
                VMEM((2, 2) + c_plane, F32),
                rows,
            ],
            flops=pair * 8,
        )(halo, xv[four], x1[two], d2[two_d], g1[:, two], mask[:, four], ct[four], mf, mb)

    send_lo, dx_lo, d1_lo, t1_lo, t2_lo = edge(True, below)
    send_hi, dx_hi, d1_hi, t1_hi, t2_hi = edge(False, above)
    from_above = lax.ppermute(send_lo, "slab", down)
    from_below = lax.ppermute(send_hi, "slab", up)

    local = call_one(fold_kernel, shape(27 * chans // 2, 4 * outs), [VMEM((k_fwd, m_fwd), F32)])(
        t1_in, t2_in, t1_lo, t2_lo, t1_hi, t2_hi
    )
    mine = sum_over_slab(local)
    other = lax.ppermute(mine, "ex", [(0, 1), (1, 0)])
    first = lax.axis_index("ex") == 0
    bound, scaling = clip_numbers(volume, kernels)
    kernel_grad = call_one(clip_kernel, shape(*kernels.shape), [])(
        jnp.where(first, mine, other), jnp.where(first, other, mine),
        bound.reshape((1, 1)), scaling.reshape((1, 1)),
    )
    input_grad = call_one(
        functools.partial(output_kernel, zs), shape(chans, zs, hs, ws), [VMEM((2, chans * hs, ws), F32)],
        flops=pair * 4,
    )(mb, d1_lo, d1_in, d1_hi, dx_lo, dx_in, dx_hi, from_below, from_above)
    return (input_grad[None], kernel_grad)


def call_one(body, out, scratch, flops=0):
    run = call(body, [out], scratch, flops)
    return lambda *args: run(*args)[0]


def per_device(*args):
    ex, chans, zs, hs, ws = args[0].shape
    blocks = ex == 1 and lax.axis_size("ex") == 2 and chans == 16 and ws == 128
    blocks = blocks and hs % 16 == 0 and zs % 2 == 0 and zs >= 8
    peers = lax.axis_size("slab")
    if blocks and peers & (peers - 1) == 0:
        return block_device(*args)
    return plain_device(*args)


def solution(mesh):
    placed = (
        P("ex", None, "slab", None, None),
        P("ex", None, "slab", None, None),
        P("ex", None, "slab", None, None),
        P("ex"),
        P("ex"),
        P(),
    )
    return jax.shard_map(
        per_device,
        mesh=mesh,
        in_specs=placed,
        out_specs=(P("ex", None, "slab", None, None), P()),
        check_vma=False,
    )
```

```python
import functools
import jax
import jax.numpy as jnp
import numpy as np
from jax import lax
from jax.experimental import pallas as pl
from jax.experimental.pallas import tpu as pltpu
from jax.sharding import PartitionSpec as P

F32, BF16 = jnp.float32, jnp.bfloat16
PZ, PH = 2, 4
PF = 2
STEP = 8
WZ, WH = PZ + 2, PH + 2
VMEM = pltpu.VMEM


def with_halo(array, sides, width):
    for axis, dim in sides:
        peers, length = (lax.axis_size(axis), array.shape[dim])
        up = [(i, (i + 1) % peers) for i in range(peers - 1)]
        down = [(j, i) for i, j in up]
        last = lax.slice_in_dim(array, length - width, length, axis=dim)
        leading = lax.slice_in_dim(array, 0, width, axis=dim)
        before = lax.ppermute(last, axis, up)
        after = lax.ppermute(leading, axis, down)
        array = jnp.concatenate([before, array, after], axis=dim)
    return array


def shifted_stack(extended, flip):
    zs = extended.shape[2] - 2
    hs, ws = (extended.shape[3], extended.shape[4])
    padded = jnp.pad(extended, ((0, 0), (0, 0), (0, 0), (1, 1), (1, 1)))
    taps = []
    for tap in range(27):
        dz, dh, dw = tap // 9, tap // 3 % 3, tap % 3
        if flip:
            dz, dh, dw = 2 - dz, 2 - dh, 2 - dw
        taps.append(padded[:, :, dz : dz + zs, dh : dh + hs, dw : dw + ws])
    return jnp.stack(taps, axis=1)


def layer_forward(field, kernel):
    patches = shifted_stack(with_halo(field, (("slab", 2),), 1), False)
    ex, taps, chans, zs, hs, ws = patches.shape
    patches = patches.reshape((ex, taps * chans, zs, hs, ws))
    pre = jnp.einsum("ok,ekzhw->eozhw", kernel, patches, preferred_element_type=F32)
    return (pre, patches)


def layer_backward(delta, kernel, patches):
    grads = jnp.einsum("eozhw,ekzhw->eok", delta, patches, preferred_element_type=F32)
    extended = with_halo(delta, (("slab", 2),), 1)
    shaped = kernel.reshape((kernel.shape[0], 27, kernel.shape[1] // 27))
    spread = jnp.einsum(
        "otc,etozhw->eczhw", shaped, shifted_stack(extended, True), preferred_element_type=F32
    )
    return (grads, spread)


def plain_device(volume, cotangent, gate_mask, loss_scale, canary, kernels):
    chans = volume.shape[1]
    local_ex = volume.shape[0]
    mask_one = gate_mask[:, 0][:, None].astype(F32)
    mask_two = gate_mask[:, 1][:, None].astype(F32)
    pre_one, patches_one = layer_forward(volume, kernels[0])
    value_one = pre_one[:, :chans]
    sig_one = jax.nn.sigmoid(pre_one[:, chans:])
    hidden = (volume.astype(F32) + value_one * sig_one * mask_one).astype(BF16)
    pre_two, patches_two = layer_forward(hidden, kernels[1])
    value_two = pre_two[:, :chans]
    sig_two = jax.nn.sigmoid(pre_two[:, chans:])
    weights = channel_weights(chans, loss_scale, canary)
    grad_out = cotangent.astype(F32) * weights[:, :, None, None, None]
    delta_two = jnp.concatenate(
        [
            grad_out * sig_two * mask_two,
            grad_out * value_two * sig_two * (1.0 - sig_two) * mask_two,
        ],
        axis=1,
    ).astype(BF16)
    grad_two, spread_two = layer_backward(delta_two, kernels[1], patches_two)
    grad_hidden = grad_out + spread_two
    delta_one = jnp.concatenate(
        [
            grad_hidden * sig_one * mask_one,
            grad_hidden * value_one * sig_one * (1.0 - sig_one) * mask_one,
        ],
        axis=1,
    ).astype(BF16)
    grad_one, spread_one = layer_backward(delta_one, kernels[0], patches_one)
    input_grad = grad_hidden + spread_one
    flat = jnp.stack([grad_one, grad_two], axis=1).reshape((local_ex, -1))
    bound, scaling = clip_numbers(volume, kernels)
    summed = lax.psum(flat, "slab")
    norm = jnp.sqrt(jnp.sum(summed * summed, axis=1) + 1e-06)
    factor = jnp.minimum(1.0, bound / norm)
    total = lax.psum(jnp.sum(summed * factor[:, None], axis=0), "ex")
    return (input_grad, (total * scaling).reshape(kernels.shape))


def channel_weights(chans, loss_scale, canary):
    ids = jnp.arange(chans, dtype=jnp.int32)
    return (1.0 + 2.0 * (ids[None, :] == canary[:, None]).astype(F32)) * loss_scale[:, None]


def clip_numbers(volume, kernels, sqrt=jnp.sqrt, one=F32):
    chans = volume.shape[1]
    depth = volume.shape[2] * lax.axis_size("slab")
    bound = 20.0 * sqrt(one(depth * volume.shape[3] * volume.shape[4]))
    examples = volume.shape[0] * lax.axis_size("ex")
    scaling = sqrt(one(108 * chans * chans)) / (bound * sqrt(one(examples)))
    return bound, scaling


def side_shifts(tile):
    lane = lax.broadcasted_iota(jnp.int32, tile.shape, tile.ndim - 1)
    last = tile.shape[-1] - 1
    before = jnp.where(lane == 0, 0.0, pltpu.roll(tile, 1, tile.ndim - 1))
    after = jnp.where(lane == last, 0.0, pltpu.roll(tile, last, tile.ndim - 1))
    return before, after


def put_rows(ref, plane, h, tile):
    rows, chans = tile.shape[:2]
    before, after = side_shifts(tile)
    for s, part in enumerate((before, tile, after)):
        ref[plane, pl.ds(h + 1, rows), s * chans : (s + 1) * chans, :] = part.astype(BF16)


def put_half(ref, plane, h, tile, which):
    rows, chans = tile.shape[:2]
    before, after = side_shifts(tile)
    for s, part in enumerate((before, tile, after)):
        at = (s * 2 + which) * chans
        ref[plane, pl.ds(h + 1, rows), at : at + chans, :] = part.astype(BF16)


def clear_edges(ref):
    for plane in range(ref.shape[0]):
        zero = jnp.zeros(ref.shape[2:], BF16)
        ref[plane, 0] = zero
        ref[plane, ref.shape[1] - 1] = zero


def windows(planes, blocks, ph):
    cols = []
    for h in blocks:
        parts = []
        for ref, at in planes:
            part = ref[at, pl.ds(h, ph + 2)]
            parts.append(part.reshape((-1, part.shape[-1])))
        cols.append(jnp.concatenate(parts, axis=0))
    return jnp.concatenate(cols, axis=1)


def conv_blocks(mat, planes, h, ph=PH):
    out = jnp.dot(mat, windows(planes, range(h, h + STEP, ph), ph), preferred_element_type=F32)
    return out.reshape((PZ * ph, -1, out.shape[-1]))


def split_blocks(tile, fn):
    ph = tile.shape[0] // PZ
    blocks = STEP // ph
    width = tile.shape[-1] // blocks
    for pz in range(PZ):
        for b in range(blocks):
            fn(pz, b * ph, tile[pz * ph : (pz + 1) * ph, :, b * width : (b + 1) * width])


def join_blocks(fn, ph):
    planes = []
    for pz in range(PZ):
        planes.append(jnp.concatenate([fn(pz, row) for row in range(0, STEP, ph)], axis=2))
    return jnp.concatenate(planes, axis=0)


def mask_blocks(mask_planes, h, chans, ph):
    parts = []
    for pz in range(PZ):
        ref, at = mask_planes[pz]
        rows = ref[at + (pl.ds(h, STEP),)].astype(F32)
        both = jnp.concatenate([rows[row : row + ph] for row in range(0, STEP, ph)], axis=1)
        parts.append(jnp.broadcast_to(both[:, None, :], (ph, chans, both.shape[1])))
    return jnp.concatenate(parts, axis=0)


def row_loop(hs, body):
    for h in range(0, hs, STEP):
        body(h)


def forward_one(mat_ref, v_planes, v_centre, mask_planes, x1, x1_at, gates, gates_at, hs, chans):
    def body(h):
        pre = conv_blocks(mat_ref[...], v_planes, h, PF)
        val, sig = pre[:, :chans], jax.nn.sigmoid(pre[:, chans:])
        mask = mask_blocks(mask_planes, h, chans, PF)

        def centre(pz, row):
            ref, at = v_centre[pz]
            return ref[at, pl.ds(h + row + 1, PF), chans : 2 * chans, :].astype(F32)

        open_ = sig * mask
        hid = join_blocks(centre, PF) + val * open_
        slope = val * open_ * (1.0 - sig)
        split_blocks(hid, lambda pz, row, t: put_rows(x1, x1_at + pz, h + row, t))

        def keep(which):
            def put(pz, row, t):
                gates[which, gates_at + pz, pl.ds(h + row, PF)] = t

            return put

        split_blocks(open_, keep(0))
        split_blocks(slope, keep(1))

    row_loop(hs, body)


def forward_two(mat_ref, x1_planes, mask_planes, dy_fn, d2, d2_at, hs, chans):
    def body(h):
        pre = conv_blocks(mat_ref[...], x1_planes, h, PF)
        val, sig = pre[:, :chans], jax.nn.sigmoid(pre[:, chans:])
        dy = join_blocks(lambda pz, row: dy_fn(pz, h + row, PF), PF)
        top = dy * sig * mask_blocks(mask_planes, h, chans, PF)
        low = top * val * (1.0 - sig)
        split_blocks(top, lambda pz, row, t: put_half(d2, d2_at + pz, h + row, t, 0))
        split_blocks(low, lambda pz, row, t: put_half(d2, d2_at + pz, h + row, t, 1))

    row_loop(hs, body)


def backward_two(mat, d2_planes, dy_fn, gates, gates_at, dx, dx_at, d1, d1_at, hs):
    def body(h):
        def each(pz, row, part):
            row = h + row
            if dy_fn[pz] is not None:
                part = part + dy_fn[pz](row)
            dx[dx_at + pz, pl.ds(row, PH)] = part
            for which in range(2):
                gate = gates[which, gates_at + pz, pl.ds(row, PH)]
                put_half(d1, d1_at + pz, row, part * gate, which)

        split_blocks(conv_blocks(mat(), d2_planes, h), each)

    row_loop(hs, body)


def weight_blocks(x_planes, d_planes, acc, hs):
    blocks = tuple(range(0, hs, PH))
    lhs = windows(x_planes, blocks, PH)
    cols = []
    for h in blocks:
        parts = []
        for ref, at in d_planes:
            outs = ref.shape[2] // 3
            parts.append(ref[at, h + 1 : h + 1 + PH, outs : 2 * outs, :].reshape((PH * outs, -1)))
        cols.append(jnp.concatenate(parts, axis=0))
    rhs = jnp.concatenate(cols, axis=1)
    acc[...] += lax.dot_general(lhs, rhs, (((1,), (1,)), ((), ())), preferred_element_type=F32)


def fold_blocks(acc, outs, chans):
    taps = 9 * chans
    width = PH * outs
    rows = WH * 3 * chans
    total = None
    for ph in range(PH):
        part = None
        for pz in range(PZ):
            pieces = []
            for dz in range(3):
                at = (pz + dz) * rows + ph * 3 * chans
                pieces.append(acc[at : at + taps, pz * width : (pz + 1) * width])
            piece = jnp.concatenate(pieces, axis=0)
            part = piece if part is None else part + piece
        if ph:
            part = pltpu.roll(part, width - ph * outs, 1)
        total = part if total is None else total + part
    return total


def place_matrix(cols, stride, total, piece):
    k = lax.broadcasted_iota(jnp.int32, (cols, total), 0)
    j = lax.broadcasted_iota(jnp.int32, (cols, total), 1)
    group = (k >= piece).astype(jnp.int32) + (k >= 2 * piece).astype(jnp.int32)
    return (j == k + group * (stride - piece)).astype(F32).astype(BF16)


def spread_kernel(rows, out_ref, layer, width, ph):
    outs, cols = rows.shape
    stride = (ph + 2) * width
    place = place_matrix(cols, stride, WZ * stride, 3 * width)
    base = jnp.dot(rows, place, preferred_element_type=F32)
    for pz in range(PZ):
        for p in range(ph):
            at = (pz * ph + p) * outs
            shift = pz * stride + p * width
            tile = pltpu.roll(base, shift, 1) if shift else base
            out_ref[layer, at : at + outs, :] = tile.astype(BF16)


def to_rows(source, scratch, put):
    chans, hs, ws = source.shape
    scratch[...] = source.astype(F32).reshape((chans * hs, ws))
    for h in range(hs):
        put(h, scratch[pl.ds(h, chans, stride=hs), :])


def flip_kernel(kernel, chans):
    turned = kernel.astype(F32).T
    pieces = [turned[t * chans : (t + 1) * chans] for t in reversed(range(27))]
    return jnp.concatenate(pieces, axis=1).astype(BF16)


def folded(acc, chans):
    outs = 2 * chans
    one, two = (fold_blocks(acc.at[layer], outs, chans) for layer in range(2))
    lane = lax.broadcasted_iota(jnp.int32, one.shape, 1)
    both = jnp.where(lane < outs, one, pltpu.roll(two, outs, 1))
    half = both.shape[0] // 2
    lane = lax.broadcasted_iota(jnp.int32, (half, both.shape[1]), 1)
    return jnp.where(lane < 2 * outs, both[:half], pltpu.roll(both[half:], 2 * outs, 1))


def pack_kernel(vol, mask, up, down):
    chans, zs = vol.shape[1:3]
    for out, first, edge in ((up, zs - 2, zs - 1), (down, 0, 0)):
        for i in range(2):
            out[i * chans : (i + 1) * chans] = vol[0, :, first + i]
        out[2 * chans] = mask[0, 0, edge].astype(F32).astype(BF16)


def arrange_kernel(vol, xv, rows):
    clear_edges(xv)

    def arrange(z, carry):
        to_rows(vol[0, :, z], rows, lambda h, t: put_rows(xv, z, h, t[None]))
        return carry

    lax.fori_loop(0, xv.shape[0], arrange, 0)


def first_kernel(xv, cot, mask, scale, canary, ker, mf, mb, ct, x1, g1, d2, total, rows, acc):
    chans, zs, hs, ws = cot.shape[1:]
    for layer in range(2):
        spread_kernel(ker[layer], mf, layer, 3 * chans, PF)
        spread_kernel(flip_kernel(ker[layer], chans), mb, layer, 6 * chans, PH)
    clear_edges(x1)
    clear_edges(d2)
    ids = lax.broadcasted_iota(jnp.int32, (chans, ws), 0)
    weights = jnp.where(ids == canary[...], 3.0, 1.0) * scale[...]

    def scaled(z, carry):
        def put(h, t):
            ct[z, h] = t * weights

        to_rows(cot[0, :, z], rows, put)
        return carry

    lax.fori_loop(0, zs, scaled, 0)

    def layer_one(k, carry):
        z = 2 * k + 1
        forward_one(
            mf.at[0],
            [(xv, z - 1 + i) for i in range(WZ)],
            [(xv, z + i) for i in range(PZ)],
            [(mask, (0, 0, z + i)) for i in range(PZ)],
            x1, 2 * k, g1, 2 * k, hs, chans,
        )
        return carry

    lax.fori_loop(0, (zs - 2) // 2, layer_one, 0)
    acc[...] = jnp.zeros_like(acc)

    def layer_two(k, carry):
        z = 2 * k + 2
        x_planes = [(x1, z - 2 + i) for i in range(WZ)]
        forward_two(
            mf.at[1], x_planes, [(mask, (0, 1, z + i)) for i in range(PZ)],
            lambda pz, h, n: ct[z + pz, pl.ds(h, n)], d2, z, hs, chans,
        )
        weight_blocks(x_planes, two(d2, z), acc.at[1], hs)
        return carry

    lax.fori_loop(0, (zs - 4) // 2, layer_two, 0)
    total[...] = folded(acc, chans)


def two(ref, at):
    return [(ref, at), (ref, at + 1)]


def edge_parts(low, halo, xv, x1, mask, ct, mf, mb, send, dx, d1, d2, d2_at, xh, x1h, gh, rows, acc):
    zs, chans, hs = xv.shape[0], xv.shape[2] // 3, xv.shape[1] - 2
    clear_edges(xh)
    clear_edges(x1h)
    for i in range(2):
        to_rows(halo[i * chans : (i + 1) * chans], rows, lambda h, t: put_rows(xh, i, h, t[None]))
    outer = (halo, (2 * chans,))
    if low:
        v_planes = two(xh, 0) + two(xv, 0)
        masks1 = [outer, (mask, (0, 0, 0))]
        x_planes = two(x1h, 0) + two(x1, 0)
        half = slice(mb.shape[2] // 2, mb.shape[2])
        dys = [None, lambda h: ct[0, pl.ds(h, PH)]]
        first, outside = 0, 0
    else:
        v_planes = two(xv, zs - 2) + two(xh, 0)
        masks1 = [(mask, (0, 0, zs - 1)), outer]
        x_planes = two(x1, zs - 4) + two(x1h, 0)
        half = slice(0, mb.shape[2] // 2)
        dys = [lambda h: ct[zs - 1, pl.ds(h, PH)], None]
        first, outside = zs - 2, 1
    masks2 = [(mask, (0, 1, first + i)) for i in range(PZ)]
    forward_one(mf.at[0], v_planes, v_planes[1:3], masks1, x1h, 0, gh, 0, hs, chans)
    forward_two(
        mf.at[1], x_planes, masks2, lambda pz, h, n: ct[first + pz, pl.ds(h, n)], d2, d2_at, hs, chans
    )
    backward_two(lambda: mb[1, :, half], two(d2, d2_at), dys, gh, 0, dx, 0, d1, 0, hs)

    def spread(h):
        def each(pz, row, part):
            if pz == 1 - outside:
                part = part + dx[outside, pl.ds(h + row, PH)]
            send[pz, pl.ds(h + row, PH)] = part.astype(BF16)

        split_blocks(conv_blocks(mb[0, :, half], two(d1, 0), h), each)

    row_loop(hs, spread)
    acc[...] = jnp.zeros_like(acc)
    weight_blocks(x_planes, two(d2, d2_at), acc.at[1], hs)
    weight_blocks(v_planes, two(d1, 0), acc.at[0], hs)


def low_kernel(halo, xv, x1, mask, ct, mf, mb, before, d2_in, send, dx, d1, d2, total, xh, x1h, gh, rows, acc):
    clear_edges(d1)
    edge_parts(True, halo, xv, x1, mask, ct, mf, mb, send, dx, d1, d2, 0, xh, x1h, gh, rows, acc)
    total[...] = before[...] + folded(acc, xv.shape[2] // 3)


def middle_kernel(xv, g1, ct, mb, d2, before, dx, d1, total, acc):
    zs, chans, hs = xv.shape[0], xv.shape[2] // 3, xv.shape[1] - 2
    clear_edges(d1)
    acc[...] = jnp.zeros_like(acc)

    def layer_back(k, carry):
        z = 2 * k + 1
        dys = [lambda h, i=i: ct[z + i, pl.ds(h, PH)] for i in range(PZ)]
        backward_two(
            lambda: mb[1], [(d2, z - 1 + i) for i in range(WZ)], dys, g1, z - 1, dx, 2 * k, d1, 2 * k, hs
        )
        weight_blocks([(xv, z - 1 + i) for i in range(WZ)], two(d1, 2 * k), acc.at[0], hs)
        return carry

    lax.fori_loop(0, (zs - 4) // 2, layer_back, 0)
    total[...] = before[...] + folded(acc, chans)


def high_kernel(halo, xv, x1, g1, mask, ct, mf, mb, d2, before,
                send, dx, d1, dxn, d1n, total, xh, x1h, d2h, gh, rows, acc):
    zs, chans, hs = xv.shape[0], xv.shape[2] // 3, xv.shape[1] - 2
    for ref in (d1, d1n, d2h):
        clear_edges(ref)
    edge_parts(False, halo, xv, x1, mask, ct, mf, mb, send, dx, d1, d2h, 0, xh, x1h, gh, rows, acc)
    z = zs - 3
    dys = [lambda h, i=i: ct[z + i, pl.ds(h, PH)] for i in range(PZ)]
    backward_two(lambda: mb[1], two(d2, zs - 4) + two(d2h, 0), dys, g1, z - 1, dxn, 0, d1n, 0, hs)
    weight_blocks([(xv, z - 1 + i) for i in range(WZ)], two(d1n, 0), acc.at[0], hs)
    total[...] = before[...] + folded(acc, chans)


def output_kernel(picks, extra_at, mb, *refs):
    out, token, rows = refs[-3:]
    extra = None if extra_at is None else refs[extra_at]
    chans, hs, ws = out.shape[1], out.shape[3], out.shape[4]
    d_planes = [(refs[i], at) for i, at in picks[:WZ]]
    dxs = [(refs[i], at) for i, at in picks[WZ:]]

    def body(h):
        def each(pz, row, part):
            row = h + row
            ref, at = dxs[pz]
            part = part + ref[at, pl.ds(row, PH)]
            if extra is not None:
                part = part + extra[pz, pl.ds(row, PH)].astype(F32)
            rows[pz, pl.ds(row * chans, PH * chans), :] = part.reshape((PH * chans, ws))

        split_blocks(conv_blocks(mb[0], d_planes, h), each)

    row_loop(hs, body)
    for pz in range(PZ):
        for c in range(chans):
            out[0, c, pz] = rows[pz, pl.ds(c, hs, stride=chans), :]
    token[...] = rows[0, :8, :]


def clip_kernel(bound, scaling, mine, other, out):
    total = None
    for ref in (mine, other):
        value = ref[...]
        norm = jnp.sqrt(jnp.sum(value * value, keepdims=True) + 1e-06)
        part = value * jnp.minimum(1.0, bound / norm)
        total = part if total is None else total + part
    total = total * scaling
    outs = out.shape[1]
    half = total.shape[0]
    flat = total.T
    for layer in range(2):
        for part in range(2):
            at = (part * 2 + layer) * outs
            out[layer, :, part * half : (part + 1) * half] = flat[at : at + outs]


def call(body, outs, scratch=(), flops=0, vmem=16 << 20, scalars=(), aliases=()):
    def run(*args):
        size = sum(a.size * a.dtype.itemsize for a in args) + sum(o.size * o.dtype.itemsize for o in outs)
        spaces = [pltpu.SMEM if i in scalars else VMEM for i in range(len(args))]
        return pl.pallas_call(
            body,
            out_shape=outs,
            in_specs=[pl.BlockSpec(memory_space=space) for space in spaces],
            scratch_shapes=list(scratch),
            input_output_aliases=dict(aliases),
            compiler_params=pltpu.CompilerParams(vmem_limit_bytes=vmem),
            cost_estimate=pl.CostEstimate(flops=flops, bytes_accessed=size, transcendentals=0),
        )(*args)

    return run


def shape(*dims, dtype=F32):
    return jax.ShapeDtypeStruct(dims, dtype)


def output_planes(like, z, mb, d_planes, dxs, extra, buffer, after, flops=0):
    chans, zs, hs, ws = like.shape[1:]
    arrays, picks = [], []
    for array, at in d_planes + dxs:
        where = [i for i, a in enumerate(arrays) if a is array]
        if not where:
            arrays.append(array)
        picks.append((where[0] if where else len(arrays) - 1, at))
    operands = [mb] + arrays + ([] if extra is None else [extra])
    specs = [pl.BlockSpec(memory_space=VMEM)] * len(operands)
    unread = after if buffer is None else after + [buffer]
    aliases = {} if buffer is None else {len(operands) + len(after): 0}
    body = functools.partial(output_kernel, tuple(picks), None if extra is None else len(arrays))
    return pl.pallas_call(
        body,
        grid=(1,),
        out_shape=[shape(*like.shape), shape(8, ws)],
        in_specs=specs + [pl.BlockSpec(memory_space=pl.ANY)] * len(unread),
        out_specs=[
            pl.BlockSpec((1, chans, PZ, hs, ws), lambda i: (0, 0, z // PZ, 0, 0)),
            pl.BlockSpec(memory_space=VMEM),
        ],
        scratch_shapes=[VMEM((PZ, chans * hs, ws), F32)],
        input_output_aliases=aliases,
        compiler_params=pltpu.CompilerParams(vmem_limit_bytes=16 << 20),
        cost_estimate=pl.CostEstimate(flops=flops, bytes_accessed=0, transcendentals=0),
    )(*operands, *unread)


def add_kernel(mine, other, *refs):
    refs[-1][...] = mine[...] + other[...]


def add_after(mine, other, tokens):
    return pl.pallas_call(
        add_kernel,
        out_shape=shape(*mine.shape),
        in_specs=[pl.BlockSpec(memory_space=VMEM)] * 2 + [pl.BlockSpec(memory_space=pl.ANY)] * len(tokens),
        out_specs=pl.BlockSpec(memory_space=VMEM),
        compiler_params=pltpu.CompilerParams(vmem_limit_bytes=4 << 20),
    )(mine, other, *tokens)


def block_device(volume, cotangent, gate_mask, loss_scale, canary, kernels):
    chans, zs, hs, ws = volume.shape[1:]
    outs = 2 * chans
    peers = lax.axis_size("slab")
    up = [(i, i + 1) for i in range(peers - 1)]
    down = [(i + 1, i) for i in range(peers - 1)]

    payload = shape(2 * chans + 1, hs, ws, dtype=BF16)
    going_up, going_down = call(pack_kernel, [payload, payload])(volume, gate_mask)
    below = lax.ppermute(going_up, "slab", up)
    above = lax.ppermute(going_down, "slab", down)

    k_fwd, k_bwd = WZ * (PF + 2) * 3 * chans, WZ * WH * 3 * outs
    m_fwd, m_bwd = PZ * PF * outs, PZ * PH * chans
    x_plane, d_plane, c_plane = (hs + 2, 3 * chans, ws), (hs + 2, 3 * outs, ws), (hs, chans, ws)
    total = shape(27 * chans // 2, 4 * outs)
    rows = VMEM((chans * hs, ws), F32)
    acc = VMEM((2, WZ * WH * 3 * chans, PZ * PH * outs), F32)
    pair = 2 * k_bwd * m_bwd * hs // PH * ws

    def d_planes(n):
        return shape(n, *d_plane, dtype=BF16)

    (xv,) = call(arrange_kernel, [shape(zs, *x_plane, dtype=BF16)], [rows], flops=pair * 4)(volume)
    mf, mb, ct, x1, g1, d2_in, total_in = call(
        first_kernel,
        [
            shape(2, m_fwd, k_fwd, dtype=BF16),
            shape(2, m_bwd, k_bwd, dtype=BF16),
            shape(zs, *c_plane),
            shape(zs - 2, *x_plane, dtype=BF16),
            shape(2, zs - 2, *c_plane),
            d_planes(zs - 2),
            total,
        ],
        [rows, acc],
        flops=pair * 6,
    )(xv, cotangent, gate_mask, loss_scale.reshape((1, 1)), canary.reshape((1, 1)), kernels)

    halos = [VMEM((2,) + x_plane, BF16), VMEM((2,) + x_plane, BF16)]
    gates = VMEM((2, 2) + c_plane, F32)
    send_lo, dx_lo, d1_lo, d2_lo, total_lo = call(
        low_kernel,
        [shape(2, *c_plane, dtype=BF16), shape(2, *c_plane), d_planes(2), d_planes(zs - 2), total],
        halos + [gates, rows, acc],
        flops=pair * 5,
        aliases={8: 3},
    )(below, xv, x1, gate_mask, ct, mf, mb, total_in, d2_in)
    from_above = lax.ppermute(send_lo, "slab", down)
    dx_in, d1_in, total_in = call(
        middle_kernel,
        [shape(zs - 4, *c_plane), d_planes(zs - 4), total],
        [acc],
        flops=pair * 4,
    )(xv, g1, ct, mb, d2_lo, total_lo)
    send_hi, dx_hi, d1_hi, dx_hn, d1_hn, total_hi = call(
        high_kernel,
        [
            shape(2, *c_plane, dtype=BF16),
            shape(2, *c_plane), d_planes(2), shape(2, *c_plane), d_planes(2), total,
        ],
        halos + [VMEM((2,) + d_plane, BF16), gates, rows, acc],
        flops=pair * 7,
    )(above, xv, x1, g1, gate_mask, ct, mf, mb, d2_lo, total_in)
    from_below = lax.ppermute(send_hi, "slab", up)

    def place(lo, mid, hn, hi, z):
        if z <= 0:
            return (lo, z + 1)
        if z <= zs - 4:
            return (mid, z - 1)
        return (hn, z - (zs - 3)) if z <= zs - 2 else (hi, z - (zs - 1))

    inner = list(range(2, zs - 2, 2))
    buffer = None
    mine = total_hi
    steps = [1 << i for i in range(peers.bit_length() - 1)]
    steps = steps[1:] + steps[:1]
    jobs = inner + [zs - 2, 0]
    waits = {0: [from_above]}
    for place_in_order, step in enumerate(steps):
        other = lax.ppermute(mine, "slab", [(i, i ^ step) for i in range(peers)])
        left = len(steps) - place_in_order
        now, jobs = jobs[: -(-len(jobs) // left)], jobs[-(-len(jobs) // left) :]
        tokens = []
        for z in now:
            d_list = [place(d1_lo, d1_in, d1_hn, d1_hi, z - 1 + i) for i in range(WZ)]
            dx_list = [place(dx_lo, dx_in, dx_hn, dx_hi, z + i) for i in range(PZ)]
            extra = from_above if z == zs - 2 else from_below if z == 0 else None
            buffer, token = output_planes(volume, z, mb, d_list, dx_list, extra, buffer, [mine] + waits.get(place_in_order, []))
            tokens.append(token)
        mine = add_after(mine, other, tokens)
    other = lax.ppermute(mine, "ex", [(0, 1), (1, 0)])
    numbers = [float(n) for n in clip_numbers(volume, kernels, np.sqrt, np.float32)]
    kernel_grad = call_one(functools.partial(clip_kernel, *numbers), shape(*kernels.shape), [])(mine, other)
    return (buffer, kernel_grad)


def call_one(body, out, scratch, **kwargs):
    run = call(body, [out], scratch, **kwargs)
    return lambda *args: run(*args)[0]


def per_device(*args):
    ex, chans, zs, hs, ws = args[0].shape
    blocks = ex == 1 and lax.axis_size("ex") == 2 and chans == 16 and ws == 128
    blocks = blocks and hs % 16 == 0 and zs % 2 == 0 and zs >= 8
    peers = lax.axis_size("slab")
    if blocks and peers & (peers - 1) == 0:
        return block_device(*args)
    return plain_device(*args)


def solution(mesh):
    placed = (
        P("ex", None, "slab", None, None),
        P("ex", None, "slab", None, None),
        P("ex", None, "slab", None, None),
        P("ex"),
        P("ex"),
        P(),
    )
    return jax.shard_map(
        per_device,
        mesh=mesh,
        in_specs=placed,
        out_specs=(P("ex", None, "slab", None, None), P()),
        check_vma=False,
    )
```

```python
import functools
import jax
import jax.numpy as jnp
import numpy as np
from jax import lax
from jax.experimental import pallas as pl
from jax.experimental.pallas import tpu as pltpu
from jax.sharding import PartitionSpec as P

F32, BF16 = jnp.float32, jnp.bfloat16
PZ, PH = 2, 4
PF = 2
STEP = 8
WZ, WH = PZ + 2, PH + 2
VMEM = pltpu.VMEM


def with_halo(array, sides, width):
    for axis, dim in sides:
        peers, length = (lax.axis_size(axis), array.shape[dim])
        up = [(i, (i + 1) % peers) for i in range(peers - 1)]
        down = [(j, i) for i, j in up]
        last = lax.slice_in_dim(array, length - width, length, axis=dim)
        leading = lax.slice_in_dim(array, 0, width, axis=dim)
        before = lax.ppermute(last, axis, up)
        after = lax.ppermute(leading, axis, down)
        array = jnp.concatenate([before, array, after], axis=dim)
    return array


def shifted_stack(extended, flip):
    zs = extended.shape[2] - 2
    hs, ws = (extended.shape[3], extended.shape[4])
    padded = jnp.pad(extended, ((0, 0), (0, 0), (0, 0), (1, 1), (1, 1)))
    taps = []
    for tap in range(27):
        dz, dh, dw = tap // 9, tap // 3 % 3, tap % 3
        if flip:
            dz, dh, dw = 2 - dz, 2 - dh, 2 - dw
        taps.append(padded[:, :, dz : dz + zs, dh : dh + hs, dw : dw + ws])
    return jnp.stack(taps, axis=1)


def layer_forward(field, kernel):
    patches = shifted_stack(with_halo(field, (("slab", 2),), 1), False)
    ex, taps, chans, zs, hs, ws = patches.shape
    patches = patches.reshape((ex, taps * chans, zs, hs, ws))
    pre = jnp.einsum("ok,ekzhw->eozhw", kernel, patches, preferred_element_type=F32)
    return (pre, patches)


def layer_backward(delta, kernel, patches):
    grads = jnp.einsum("eozhw,ekzhw->eok", delta, patches, preferred_element_type=F32)
    extended = with_halo(delta, (("slab", 2),), 1)
    shaped = kernel.reshape((kernel.shape[0], 27, kernel.shape[1] // 27))
    spread = jnp.einsum(
        "otc,etozhw->eczhw", shaped, shifted_stack(extended, True), preferred_element_type=F32
    )
    return (grads, spread)


def plain_device(volume, cotangent, gate_mask, loss_scale, canary, kernels):
    chans = volume.shape[1]
    local_ex = volume.shape[0]
    mask_one = gate_mask[:, 0][:, None].astype(F32)
    mask_two = gate_mask[:, 1][:, None].astype(F32)
    pre_one, patches_one = layer_forward(volume, kernels[0])
    value_one = pre_one[:, :chans]
    sig_one = jax.nn.sigmoid(pre_one[:, chans:])
    hidden = (volume.astype(F32) + value_one * sig_one * mask_one).astype(BF16)
    pre_two, patches_two = layer_forward(hidden, kernels[1])
    value_two = pre_two[:, :chans]
    sig_two = jax.nn.sigmoid(pre_two[:, chans:])
    weights = channel_weights(chans, loss_scale, canary)
    grad_out = cotangent.astype(F32) * weights[:, :, None, None, None]
    delta_two = jnp.concatenate(
        [
            grad_out * sig_two * mask_two,
            grad_out * value_two * sig_two * (1.0 - sig_two) * mask_two,
        ],
        axis=1,
    ).astype(BF16)
    grad_two, spread_two = layer_backward(delta_two, kernels[1], patches_two)
    grad_hidden = grad_out + spread_two
    delta_one = jnp.concatenate(
        [
            grad_hidden * sig_one * mask_one,
            grad_hidden * value_one * sig_one * (1.0 - sig_one) * mask_one,
        ],
        axis=1,
    ).astype(BF16)
    grad_one, spread_one = layer_backward(delta_one, kernels[0], patches_one)
    input_grad = grad_hidden + spread_one
    flat = jnp.stack([grad_one, grad_two], axis=1).reshape((local_ex, -1))
    bound, scaling = clip_numbers(volume, kernels)
    summed = lax.psum(flat, "slab")
    norm = jnp.sqrt(jnp.sum(summed * summed, axis=1) + 1e-06)
    factor = jnp.minimum(1.0, bound / norm)
    total = lax.psum(jnp.sum(summed * factor[:, None], axis=0), "ex")
    return (input_grad, (total * scaling).reshape(kernels.shape))


def channel_weights(chans, loss_scale, canary):
    ids = jnp.arange(chans, dtype=jnp.int32)
    return (1.0 + 2.0 * (ids[None, :] == canary[:, None]).astype(F32)) * loss_scale[:, None]


def clip_numbers(volume, kernels, sqrt=jnp.sqrt, one=F32):
    chans = volume.shape[1]
    depth = volume.shape[2] * lax.axis_size("slab")
    bound = 20.0 * sqrt(one(depth * volume.shape[3] * volume.shape[4]))
    examples = volume.shape[0] * lax.axis_size("ex")
    scaling = sqrt(one(108 * chans * chans)) / (bound * sqrt(one(examples)))
    return bound, scaling


def side_shifts(tile):
    lane = lax.broadcasted_iota(jnp.int32, tile.shape, tile.ndim - 1)
    last = tile.shape[-1] - 1
    before = jnp.where(lane == 0, 0.0, pltpu.roll(tile, 1, tile.ndim - 1))
    after = jnp.where(lane == last, 0.0, pltpu.roll(tile, last, tile.ndim - 1))
    return before, after


def put_rows(ref, plane, h, tile):
    rows, chans = tile.shape[:2]
    before, after = side_shifts(tile)
    for s, part in enumerate((before, tile, after)):
        ref[plane, pl.ds(h + 1, rows), s * chans : (s + 1) * chans, :] = part.astype(BF16)


def put_half(ref, plane, h, tile, which):
    rows, chans = tile.shape[:2]
    before, after = side_shifts(tile)
    for s, part in enumerate((before, tile, after)):
        at = (s * 2 + which) * chans
        ref[plane, pl.ds(h + 1, rows), at : at + chans, :] = part.astype(BF16)


def clear_edges(ref):
    for plane in range(ref.shape[0]):
        zero = jnp.zeros(ref.shape[2:], BF16)
        ref[plane, 0] = zero
        ref[plane, ref.shape[1] - 1] = zero


def windows(planes, blocks, ph):
    cols = []
    for h in blocks:
        parts = []
        for ref, at in planes:
            part = ref[at, pl.ds(h, ph + 2)]
            parts.append(part.reshape((-1, part.shape[-1])))
        cols.append(jnp.concatenate(parts, axis=0))
    return jnp.concatenate(cols, axis=1)


def conv_blocks(mat, planes, h, ph=PH):
    out = jnp.dot(mat, windows(planes, range(h, h + STEP, ph), ph), preferred_element_type=F32)
    return out.reshape((PZ * ph, -1, out.shape[-1]))


def split_blocks(tile, fn):
    ph = tile.shape[0] // PZ
    blocks = STEP // ph
    width = tile.shape[-1] // blocks
    for pz in range(PZ):
        for b in range(blocks):
            fn(pz, b * ph, tile[pz * ph : (pz + 1) * ph, :, b * width : (b + 1) * width])


def join_blocks(fn, ph):
    planes = []
    for pz in range(PZ):
        planes.append(jnp.concatenate([fn(pz, row) for row in range(0, STEP, ph)], axis=2))
    return jnp.concatenate(planes, axis=0)


def mask_blocks(mask_planes, h, chans, ph):
    parts = []
    for pz in range(PZ):
        ref, at = mask_planes[pz]
        rows = ref[at + (pl.ds(h, STEP),)].astype(F32)
        both = jnp.concatenate([rows[row : row + ph] for row in range(0, STEP, ph)], axis=1)
        parts.append(jnp.broadcast_to(both[:, None, :], (ph, chans, both.shape[1])))
    return jnp.concatenate(parts, axis=0)


def row_loop(hs, body):
    for h in range(0, hs, STEP):
        body(h)


def forward_one(mat_ref, v_planes, v_centre, mask_planes, x1, x1_at, gates, gates_at, hs, chans):
    def body(h):
        pre = conv_blocks(mat_ref[...], v_planes, h, PF)
        val, sig = pre[:, :chans], jax.nn.sigmoid(pre[:, chans:])
        mask = mask_blocks(mask_planes, h, chans, PF)

        def centre(pz, row):
            ref, at = v_centre[pz]
            return ref[at, pl.ds(h + row + 1, PF), chans : 2 * chans, :].astype(F32)

        open_ = sig * mask
        hid = join_blocks(centre, PF) + val * open_
        slope = val * open_ * (1.0 - sig)
        split_blocks(hid, lambda pz, row, t: put_rows(x1, x1_at + pz, h + row, t))

        def keep(which):
            def put(pz, row, t):
                gates[which, gates_at + pz, pl.ds(h + row, PF)] = t

            return put

        split_blocks(open_, keep(0))
        split_blocks(slope, keep(1))

    row_loop(hs, body)


def forward_two(mat_ref, x1_planes, mask_planes, dy_fn, d2, d2_at, hs, chans):
    def body(h):
        pre = conv_blocks(mat_ref[...], x1_planes, h, PF)
        val, sig = pre[:, :chans], jax.nn.sigmoid(pre[:, chans:])
        dy = join_blocks(lambda pz, row: dy_fn(pz, h + row, PF), PF)
        top = dy * sig * mask_blocks(mask_planes, h, chans, PF)
        low = top * val * (1.0 - sig)
        split_blocks(top, lambda pz, row, t: put_half(d2, d2_at + pz, h + row, t, 0))
        split_blocks(low, lambda pz, row, t: put_half(d2, d2_at + pz, h + row, t, 1))

    row_loop(hs, body)


def backward_two(mat, d2_planes, dy_fn, gates, gates_at, dx, dx_at, d1, d1_at, hs):
    def body(h):
        def each(pz, row, part):
            row = h + row
            if dy_fn[pz] is not None:
                part = part + dy_fn[pz](row)
            dx[dx_at + pz, pl.ds(row, PH)] = part
            for which in range(2):
                gate = gates[which, gates_at + pz, pl.ds(row, PH)]
                put_half(d1, d1_at + pz, row, part * gate, which)

        split_blocks(conv_blocks(mat(), d2_planes, h), each)

    row_loop(hs, body)


def weight_blocks(x_planes, d_planes, acc, hs):
    blocks = tuple(range(0, hs, PH))
    lhs = windows(x_planes, blocks, PH)
    cols = []
    for h in blocks:
        parts = []
        for ref, at in d_planes:
            outs = ref.shape[2] // 3
            parts.append(ref[at, h + 1 : h + 1 + PH, outs : 2 * outs, :].reshape((PH * outs, -1)))
        cols.append(jnp.concatenate(parts, axis=0))
    rhs = jnp.concatenate(cols, axis=1)
    acc[...] += lax.dot_general(lhs, rhs, (((1,), (1,)), ((), ())), preferred_element_type=F32)


def fold_blocks(acc, outs, chans):
    taps = 9 * chans
    width = PH * outs
    rows = WH * 3 * chans
    total = None
    for ph in range(PH):
        part = None
        for pz in range(PZ):
            pieces = []
            for dz in range(3):
                at = (pz + dz) * rows + ph * 3 * chans
                pieces.append(acc[at : at + taps, pz * width : (pz + 1) * width])
            piece = jnp.concatenate(pieces, axis=0)
            part = piece if part is None else part + piece
        if ph:
            part = pltpu.roll(part, width - ph * outs, 1)
        total = part if total is None else total + part
    return total


def place_matrix(cols, stride, total, piece):
    k = lax.broadcasted_iota(jnp.int32, (cols, total), 0)
    j = lax.broadcasted_iota(jnp.int32, (cols, total), 1)
    group = (k >= piece).astype(jnp.int32) + (k >= 2 * piece).astype(jnp.int32)
    return (j == k + group * (stride - piece)).astype(F32).astype(BF16)


def spread_kernel(rows, out_ref, layer, width, ph):
    outs, cols = rows.shape
    stride = (ph + 2) * width
    place = place_matrix(cols, stride, WZ * stride, 3 * width)
    base = jnp.dot(rows, place, preferred_element_type=F32)
    for pz in range(PZ):
        for p in range(ph):
            at = (pz * ph + p) * outs
            shift = pz * stride + p * width
            tile = pltpu.roll(base, shift, 1) if shift else base
            out_ref[layer, at : at + outs, :] = tile.astype(BF16)


def to_rows(source, scratch, put):
    chans, hs, ws = source.shape
    scratch[...] = source.astype(F32).reshape((chans * hs, ws))
    for h in range(hs):
        put(h, scratch[pl.ds(h, chans, stride=hs), :])


def flip_kernel(kernel, chans):
    turned = kernel.astype(F32).T
    pieces = [turned[t * chans : (t + 1) * chans] for t in reversed(range(27))]
    return jnp.concatenate(pieces, axis=1).astype(BF16)


def folded(acc, chans):
    outs = 2 * chans
    one, two = (fold_blocks(acc.at[layer], outs, chans) for layer in range(2))
    lane = lax.broadcasted_iota(jnp.int32, one.shape, 1)
    both = jnp.where(lane < outs, one, pltpu.roll(two, outs, 1))
    half = both.shape[0] // 2
    lane = lax.broadcasted_iota(jnp.int32, (half, both.shape[1]), 1)
    return jnp.where(lane < 2 * outs, both[:half], pltpu.roll(both[half:], 2 * outs, 1))


def pack_kernel(first, edge, vol, mask, *refs):
    out, chans = refs[-1], vol.shape[1]
    for i in range(2):
        out[i * chans : (i + 1) * chans] = vol[0, :, first + i]
    out[2 * chans] = mask[0, 0, edge].astype(F32).astype(BF16)


def arrange_kernel(vol, xv, rows):
    clear_edges(xv)

    def arrange(z, carry):
        to_rows(vol[0, :, z], rows, lambda h, t: put_rows(xv, z, h, t[None]))
        return carry

    lax.fori_loop(0, xv.shape[0], arrange, 0)


def first_kernel(xv, cot, mask, weights, ker, mf, mb, ct, x1, g1, d2, total, rows, acc):
    chans, zs, hs, ws = cot.shape[1:]
    for layer in range(2):
        spread_kernel(ker[layer], mf, layer, 3 * chans, PF)
        spread_kernel(flip_kernel(ker[layer], chans), mb, layer, 6 * chans, PH)
    clear_edges(x1)
    clear_edges(d2)

    def scaled(z, carry):
        def put(h, t):
            ct[z, h] = t * weights[...]

        to_rows(cot[0, :, z], rows, put)
        return carry

    lax.fori_loop(0, zs, scaled, 0)

    def layer_one(k, carry):
        z = 2 * k + 1
        forward_one(
            mf.at[0],
            [(xv, z - 1 + i) for i in range(WZ)],
            [(xv, z + i) for i in range(PZ)],
            [(mask, (0, 0, z + i)) for i in range(PZ)],
            x1, 2 * k, g1, 2 * k, hs, chans,
        )
        return carry

    lax.fori_loop(0, (zs - 2) // 2, layer_one, 0)
    acc[...] = jnp.zeros_like(acc)

    def layer_two(k, carry):
        z = 2 * k + 2
        x_planes = [(x1, z - 2 + i) for i in range(WZ)]
        forward_two(
            mf.at[1], x_planes, [(mask, (0, 1, z + i)) for i in range(PZ)],
            lambda pz, h, n: ct[z + pz, pl.ds(h, n)], d2, z, hs, chans,
        )
        weight_blocks(x_planes, two(d2, z), acc.at[1], hs)
        return carry

    lax.fori_loop(0, (zs - 4) // 2, layer_two, 0)
    total[...] = folded(acc, chans)


def two(ref, at):
    return [(ref, at), (ref, at + 1)]


def edge_parts(low, halo, xv, x1, mask, ct, mf, mb, send, dx, d1, d2, d2_at, xh, x1h, gh, rows, acc):
    zs, chans, hs = xv.shape[0], xv.shape[2] // 3, xv.shape[1] - 2
    clear_edges(xh)
    clear_edges(x1h)
    for i in range(2):
        to_rows(halo[i * chans : (i + 1) * chans], rows, lambda h, t: put_rows(xh, i, h, t[None]))
    outer = (halo, (2 * chans,))
    if low:
        v_planes = two(xh, 0) + two(xv, 0)
        masks1 = [outer, (mask, (0, 0, 0))]
        x_planes = two(x1h, 0) + two(x1, 0)
        half = slice(mb.shape[2] // 2, mb.shape[2])
        dys = [None, lambda h: ct[0, pl.ds(h, PH)]]
        first, outside = 0, 0
    else:
        v_planes = two(xv, zs - 2) + two(xh, 0)
        masks1 = [(mask, (0, 0, zs - 1)), outer]
        x_planes = two(x1, zs - 4) + two(x1h, 0)
        half = slice(0, mb.shape[2] // 2)
        dys = [lambda h: ct[zs - 1, pl.ds(h, PH)], None]
        first, outside = zs - 2, 1
    masks2 = [(mask, (0, 1, first + i)) for i in range(PZ)]
    forward_one(mf.at[0], v_planes, v_planes[1:3], masks1, x1h, 0, gh, 0, hs, chans)
    forward_two(
        mf.at[1], x_planes, masks2, lambda pz, h, n: ct[first + pz, pl.ds(h, n)], d2, d2_at, hs, chans
    )
    backward_two(lambda: mb[1, :, half], two(d2, d2_at), dys, gh, 0, dx, 0, d1, 0, hs)

    def spread(h):
        def each(pz, row, part):
            if pz == 1 - outside:
                part = part + dx[outside, pl.ds(h + row, PH)]
            send[pz, pl.ds(h + row, PH)] = part.astype(BF16)

        split_blocks(conv_blocks(mb[0, :, half], two(d1, 0), h), each)

    row_loop(hs, spread)
    acc[...] = jnp.zeros_like(acc)
    weight_blocks(x_planes, two(d2, d2_at), acc.at[1], hs)
    weight_blocks(v_planes, two(d1, 0), acc.at[0], hs)


def low_kernel(halo, xv, x1, mask, ct, mf, mb, before, d2_in, send, dx, d1, d2, total, xh, x1h, gh, rows, acc):
    clear_edges(d1)
    edge_parts(True, halo, xv, x1, mask, ct, mf, mb, send, dx, d1, d2, 0, xh, x1h, gh, rows, acc)
    total[...] = before[...] + folded(acc, xv.shape[2] // 3)


def middle_kernel(xv, g1, ct, mb, d2, before, passing, dx, d1, total, passed, acc):
    zs, chans, hs = xv.shape[0], xv.shape[2] // 3, xv.shape[1] - 2
    clear_edges(d1)
    acc[...] = jnp.zeros_like(acc)

    def layer_back(k, carry):
        z = 2 * k + 1
        dys = [lambda h, i=i: ct[z + i, pl.ds(h, PH)] for i in range(PZ)]
        backward_two(
            lambda: mb[1], [(d2, z - 1 + i) for i in range(WZ)], dys, g1, z - 1, dx, 2 * k, d1, 2 * k, hs
        )
        weight_blocks([(xv, z - 1 + i) for i in range(WZ)], two(d1, 2 * k), acc.at[0], hs)
        return carry

    lax.fori_loop(0, (zs - 4) // 2, layer_back, 0)
    total[...] = before[...] + folded(acc, chans)


def high_kernel(halo, xv, x1, g1, mask, ct, mf, mb, d2, before,
                send, dx, d1, dxn, d1n, total, xh, x1h, d2h, gh, rows, acc):
    zs, chans, hs = xv.shape[0], xv.shape[2] // 3, xv.shape[1] - 2
    for ref in (d1, d1n, d2h):
        clear_edges(ref)
    edge_parts(False, halo, xv, x1, mask, ct, mf, mb, send, dx, d1, d2h, 0, xh, x1h, gh, rows, acc)
    z = zs - 3
    dys = [lambda h, i=i: ct[z + i, pl.ds(h, PH)] for i in range(PZ)]
    backward_two(lambda: mb[1], two(d2, zs - 4) + two(d2h, 0), dys, g1, z - 1, dxn, 0, d1n, 0, hs)
    weight_blocks([(xv, z - 1 + i) for i in range(WZ)], two(d1n, 0), acc.at[0], hs)
    total[...] = before[...] + folded(acc, chans)


def output_kernel(picks, extra_at, mb, *refs):
    out, token, rows = refs[-3:]
    extra = None if extra_at is None else refs[extra_at]
    chans, hs, ws = out.shape[1], out.shape[3], out.shape[4]
    d_planes = [(refs[i], at) for i, at in picks[:WZ]]
    dxs = [(refs[i], at) for i, at in picks[WZ:]]

    def body(h):
        def each(pz, row, part):
            row = h + row
            ref, at = dxs[pz]
            part = part + ref[at, pl.ds(row, PH)]
            if extra is not None:
                part = part + extra[pz, pl.ds(row, PH)].astype(F32)
            rows[pz, pl.ds(row * chans, PH * chans), :] = part.reshape((PH * chans, ws))

        split_blocks(conv_blocks(mb[0], d_planes, h), each)

    row_loop(hs, body)
    for pz in range(PZ):
        for c in range(chans):
            out[0, c, pz] = rows[pz, pl.ds(c, hs, stride=chans), :]
    token[...] = rows[0, :8, :]


def clip_kernel(bound, scaling, mine, other, out):
    total = None
    for ref in (mine, other):
        value = ref[...]
        norm = jnp.sqrt(jnp.sum(value * value, keepdims=True) + 1e-06)
        part = value * jnp.minimum(1.0, bound / norm)
        total = part if total is None else total + part
    total = total * scaling
    outs = out.shape[1]
    half = total.shape[0]
    flat = total.T
    for layer in range(2):
        for part in range(2):
            at = (part * 2 + layer) * outs
            out[layer, :, part * half : (part + 1) * half] = flat[at : at + outs]


def call(body, outs, scratch=(), flops=0, vmem=16 << 20, aliases=(), outside=()):
    def run(*args):
        size = sum(a.size * a.dtype.itemsize for a in args) + sum(o.size * o.dtype.itemsize for o in outs)
        spaces = [pl.ANY if i in outside else VMEM for i in range(len(args))]
        return pl.pallas_call(
            body,
            out_shape=outs,
            in_specs=[pl.BlockSpec(memory_space=space) for space in spaces],
            scratch_shapes=list(scratch),
            input_output_aliases=dict(aliases),
            compiler_params=pltpu.CompilerParams(vmem_limit_bytes=vmem),
            cost_estimate=pl.CostEstimate(flops=flops, bytes_accessed=size, transcendentals=0),
        )(*args)

    return run


def shape(*dims, dtype=F32):
    return jax.ShapeDtypeStruct(dims, dtype)


def output_planes(like, z, mb, d_planes, dxs, extra, buffer, after, flops=0):
    chans, zs, hs, ws = like.shape[1:]
    arrays, picks = [], []
    for array, at in d_planes + dxs:
        where = [i for i, a in enumerate(arrays) if a is array]
        if not where:
            arrays.append(array)
        picks.append((where[0] if where else len(arrays) - 1, at))
    operands = [mb] + arrays + ([] if extra is None else [extra])
    specs = [pl.BlockSpec(memory_space=VMEM)] * len(operands)
    unread = after if buffer is None else after + [buffer]
    aliases = {} if buffer is None else {len(operands) + len(after): 0}
    body = functools.partial(output_kernel, tuple(picks), None if extra is None else len(arrays))
    return pl.pallas_call(
        body,
        grid=(1,),
        out_shape=[shape(*like.shape), shape(8, ws)],
        in_specs=specs + [pl.BlockSpec(memory_space=pl.ANY)] * len(unread),
        out_specs=[
            pl.BlockSpec((1, chans, PZ, hs, ws), lambda i: (0, 0, z // PZ, 0, 0)),
            pl.BlockSpec(memory_space=VMEM),
        ],
        scratch_shapes=[VMEM((PZ, chans * hs, ws), F32)],
        input_output_aliases=aliases,
        compiler_params=pltpu.CompilerParams(vmem_limit_bytes=16 << 20),
        cost_estimate=pl.CostEstimate(flops=flops, bytes_accessed=0, transcendentals=0),
    )(*operands, *unread)


def add_kernel(mine, other, *refs):
    refs[-1][...] = mine[...] + other[...]


def add_after(mine, other, tokens):
    return pl.pallas_call(
        add_kernel,
        out_shape=shape(*mine.shape),
        in_specs=[pl.BlockSpec(memory_space=VMEM)] * 2 + [pl.BlockSpec(memory_space=pl.ANY)] * len(tokens),
        out_specs=pl.BlockSpec(memory_space=VMEM),
        compiler_params=pltpu.CompilerParams(vmem_limit_bytes=4 << 20),
    )(mine, other, *tokens)


def block_device(volume, cotangent, gate_mask, loss_scale, canary, kernels):
    chans, zs, hs, ws = volume.shape[1:]
    outs = 2 * chans
    peers = lax.axis_size("slab")
    up = [(i, i + 1) for i in range(peers - 1)]
    down = [(i + 1, i) for i in range(peers - 1)]

    ids = lax.broadcasted_iota(jnp.int32, (chans, ws), 0)
    weights = jnp.where(ids == canary, 3.0, 1.0) * loss_scale

    def packed(first, edge, *after):
        return call_one(
            functools.partial(pack_kernel, first, edge),
            shape(2 * chans + 1, hs, ws, dtype=BF16), [],
            outside=range(2, 2 + len(after)),
        )(volume, gate_mask, *after)

    k_fwd, k_bwd = WZ * (PF + 2) * 3 * chans, WZ * WH * 3 * outs
    m_fwd, m_bwd = PZ * PF * outs, PZ * PH * chans
    x_plane, d_plane, c_plane = (hs + 2, 3 * chans, ws), (hs + 2, 3 * outs, ws), (hs, chans, ws)
    total = shape(27 * chans // 2, 4 * outs)
    rows = VMEM((chans * hs, ws), F32)
    acc = VMEM((2, WZ * WH * 3 * chans, PZ * PH * outs), F32)
    pair = 2 * k_bwd * m_bwd * hs // PH * ws

    def d_planes(n):
        return shape(n, *d_plane, dtype=BF16)

    below = lax.ppermute(packed(zs - 2, zs - 1, weights), "slab", up)
    (xv,) = call(arrange_kernel, [shape(zs, *x_plane, dtype=BF16)], [rows], flops=pair * 4)(volume)
    above = lax.ppermute(packed(0, 0, xv), "slab", down)
    mf, mb, ct, x1, g1, d2_in, total_in = call(
        first_kernel,
        [
            shape(2, m_fwd, k_fwd, dtype=BF16),
            shape(2, m_bwd, k_bwd, dtype=BF16),
            shape(zs, *c_plane),
            shape(zs - 2, *x_plane, dtype=BF16),
            shape(2, zs - 2, *c_plane),
            d_planes(zs - 2),
            total,
        ],
        [rows, acc],
        flops=pair * 6,
    )(xv, cotangent, gate_mask, weights, kernels)

    halos = [VMEM((2,) + x_plane, BF16), VMEM((2,) + x_plane, BF16)]
    gates = VMEM((2, 2) + c_plane, F32)
    send_lo, dx_lo, d1_lo, d2_lo, total_lo = call(
        low_kernel,
        [shape(2, *c_plane, dtype=BF16), shape(2, *c_plane), d_planes(2), d_planes(zs - 2), total],
        halos + [gates, rows, acc],
        flops=pair * 5,
        aliases={8: 3},
    )(below, xv, x1, gate_mask, ct, mf, mb, total_in, d2_in)
    dx_in, d1_in, total_in, send_lo = call(
        middle_kernel,
        [shape(zs - 4, *c_plane), d_planes(zs - 4), total, shape(2, *c_plane, dtype=BF16)],
        [acc],
        flops=pair * 4,
        aliases={6: 3},
    )(xv, g1, ct, mb, d2_lo, total_lo, send_lo)
    from_above = lax.ppermute(send_lo, "slab", down)
    send_hi, dx_hi, d1_hi, dx_hn, d1_hn, total_hi = call(
        high_kernel,
        [
            shape(2, *c_plane, dtype=BF16),
            shape(2, *c_plane), d_planes(2), shape(2, *c_plane), d_planes(2), total,
        ],
        halos + [VMEM((2,) + d_plane, BF16), gates, rows, acc],
        flops=pair * 7,
    )(above, xv, x1, g1, gate_mask, ct, mf, mb, d2_lo, total_in)
    from_below = lax.ppermute(send_hi, "slab", up)

    def place(lo, mid, hn, hi, z):
        if z <= 0:
            return (lo, z + 1)
        if z <= zs - 4:
            return (mid, z - 1)
        return (hn, z - (zs - 3)) if z <= zs - 2 else (hi, z - (zs - 1))

    inner = list(range(2, zs - 2, 2))
    buffer = None
    mine = total_hi
    steps = [1 << i for i in range(peers.bit_length() - 1)]
    steps = steps[1:] + steps[:1]
    jobs = inner + [zs - 2, 0]
    waits = {0: [from_above]}
    for place_in_order, step in enumerate(steps):
        other = lax.ppermute(mine, "slab", [(i, i ^ step) for i in range(peers)])
        left = len(steps) - place_in_order
        now, jobs = jobs[: -(-len(jobs) // left)], jobs[-(-len(jobs) // left) :]
        tokens = []
        for z in now:
            d_list = [place(d1_lo, d1_in, d1_hn, d1_hi, z - 1 + i) for i in range(WZ)]
            dx_list = [place(dx_lo, dx_in, dx_hn, dx_hi, z + i) for i in range(PZ)]
            extra = from_above if z == zs - 2 else from_below if z == 0 else None
            buffer, token = output_planes(volume, z, mb, d_list, dx_list, extra, buffer, [mine] + waits.get(place_in_order, []))
            tokens.append(token)
        mine = add_after(mine, other, tokens)
    other = lax.ppermute(mine, "ex", [(0, 1), (1, 0)])
    numbers = [float(n) for n in clip_numbers(volume, kernels, np.sqrt, np.float32)]
    kernel_grad = call_one(functools.partial(clip_kernel, *numbers), shape(*kernels.shape), [])(mine, other)
    return (buffer, kernel_grad)


def call_one(body, out, scratch, **kwargs):
    run = call(body, [out], scratch, **kwargs)
    return lambda *args: run(*args)[0]


def per_device(*args):
    ex, chans, zs, hs, ws = args[0].shape
    blocks = ex == 1 and lax.axis_size("ex") == 2 and chans == 16 and ws == 128
    blocks = blocks and hs % 16 == 0 and zs % 2 == 0 and zs >= 8
    peers = lax.axis_size("slab")
    if blocks and peers & (peers - 1) == 0:
        return block_device(*args)
    return plain_device(*args)


def solution(mesh):
    placed = (
        P("ex", None, "slab", None, None),
        P("ex", None, "slab", None, None),
        P("ex", None, "slab", None, None),
        P("ex"),
        P("ex"),
        P(),
    )
    return jax.shard_map(
        per_device,
        mesh=mesh,
        in_specs=placed,
        out_specs=(P("ex", None, "slab", None, None), P()),
        check_vma=False,
    )
```
